256 devices in a mesh: tm: 64 (over z, y, x_hi), query: 4 (over x_lo, core).
Axes of the slice: x: 4 (x_hi: 2, x_lo: 2; x = x_hi * 2 + x_lo), y: 4, z: 8, core: 2. Of those that a mesh axis runs over, the one named last changes fastest.
Arguments:
- series: float32 [262144], P('tm'), may hold values from -6 to 6
- tail: float32 [287], replicated, may hold values from -6 to 6
- queries: float32 [8192, 288], P(('tm', 'query')), may hold values from -6 to 6
Outputs:
- profile: float32 [262144], P('tm')
- query_profile: float32 [8192], P(('tm', 'query'))
The draws below stay inside these ranges and needn't reach their ends.
All inputs are finite; a program needn't handle non-finite values.
Results may differ from the reference program's by a relative error of at most 0.0003.
Values sent between devices are 32-bit elements; how exact they have to be, the bound alone decides.
A program may use at most 192 MiB of HBM per device.

```python
import jax
import jax.numpy as jnp
from jax import lax

M = 288
P_DEV = 4096
TAIL = 287
POSITIONS = 262144
QUERIES = 8192
N_TM = 64


def levels(own_key, dims, pieces, least, largest):
    level, own = 1.0, jax.random.fold_in(own_key, 6)
    for dim, shards_of in pieces:
        draws = jnp.exp(jax.random.uniform(jax.random.fold_in(own, dim), (shards_of,), jnp.float32, least / len(pieces), largest / len(pieces)))
        level = level * jnp.repeat(draws, dims[dim] // shards_of).reshape([-1 if axis == dim else 1 for axis in range(len(dims))])
    return level


def gaussian(rng, shape, scale, limit, split=(), kind=jnp.bfloat16):
    drawn = scale * jax.random.normal(rng, shape, jnp.float32)
    if split:
        drawn = drawn * levels(rng, shape, split, -0.22, 0.18)
    return jnp.clip(drawn, -limit, limit).astype(kind)


def setup_inputs(seed: int = 0) -> dict:
    streams_of = jax.random.split(jax.random.key(seed), 4)
    series = gaussian(streams_of[0], (POSITIONS,), 1.0, 6.0, ((0, 64),), jnp.float32)
    tail = gaussian(streams_of[1], (TAIL,), 1.0, 6.0, (), jnp.float32)
    queries = gaussian(streams_of[2], (QUERIES, M), 1.0, 6.0, ((0, 256),), jnp.float32)
    return dict(series=series, tail=tail, queries=queries)


def normalize(rows):
    mean = lax.optimization_barrier(jnp.mean(rows, axis=1, keepdims=True))
    centered = rows - mean
    sigma = jnp.sqrt(lax.optimization_barrier(jnp.mean(centered * centered, axis=1, keepdims=True)) + 1e-05)
    return centered / sigma

def reference(series, tail, queries):
    full = jnp.concatenate([series, tail])
    zq = normalize(queries)
    offsets = jnp.arange(P_DEV, dtype=jnp.int32)[:, None] + jnp.arange(M, dtype=jnp.int32)[None, :]

    def one_block(best_query, index):
        start = (index * P_DEV).astype(jnp.int32)
        piece = lax.dynamic_slice(full, (start,), (P_DEV + M - 1,))
        zt = normalize(piece[offsets])
        scores = jnp.dot(zt, zq.T, precision=lax.Precision.HIGHEST)
        value = 2.0 - 2.0 * scores / M
        return (jnp.minimum(best_query, lax.optimization_barrier(jnp.min(value, axis=0))), lax.optimization_barrier(jnp.min(value, axis=1)))
    start_best = jnp.full((QUERIES,), 8.0, jnp.float32)
    best_query, best_pos = lax.scan(one_block, start_best, jnp.arange(N_TM, dtype=jnp.int32))
    return (jnp.sqrt(best_pos.reshape(POSITIONS)), jnp.sqrt(best_query))
```

```python
import jax
import jax.numpy as jnp
from jax import lax
from jax.experimental import pallas as pl
from jax.experimental.pallas import tpu as pltpu
from jax.sharding import PartitionSpec as P

M = 288
SEG = 1024
LANES = 128
COLUMN = 32
GROUP = 8
REPLICAS = 4
REST = M - 256
MESH = pl.DeviceIdType.MESH


def split(value):
    high = value.astype(jnp.bfloat16)
    low = (value - high.astype(jnp.float32)).astype(jnp.bfloat16)
    return high, low


def hankel(row, blocks):
    r = lax.broadcasted_iota(jnp.int32, (LANES, LANES), 0)
    lane = lax.broadcasted_iota(jnp.int32, (LANES, LANES), 1)
    this = pltpu.roll(jnp.broadcast_to(row(0), (LANES, LANES)), 1, 1, stride=1, stride_axis=0)
    for u in range(blocks):
        after = pltpu.roll(jnp.broadcast_to(row(u + 1), (LANES, LANES)), 1, 1, stride=1, stride_axis=0)
        yield u, jnp.where(lane <= r, this, after)
        this = after


def kernel(
    series, tail, queries, prof, qprof,
    ext, halo, own_h, segs, bha, bla, bhb, blb, zall, zcat, acc, part, got, qpart, qgot, pall,
    halo_s, halo_r, zs, zr, ss, sr, ps, pr, qs, qr, fs, fr,
):
    tm, q = lax.axis_index("tm"), lax.axis_index("query")
    zz, yy, xh = tm // 8, (tm // 2) % 4, tm % 2
    gidx = xh * 4 + q

    def col(s, sign):
        z2 = (zz + sign * (s // 4) + 8) % 8
        y2 = (yy + sign * (s % 4) + 4) % 4
        return (z2 * 8 + y2 * 2 + xh, q)

    def grp(j, sign):
        g = (gidx + sign * j + 8) % 8
        return (tm - xh + g // 4, g % 4)

    def rep(j, sign):
        return (tm, (q + sign * j + 4) % 4)

    def remote(src, dst, send, recv, device):
        return pltpu.make_async_remote_copy(
            src_ref=src, dst_ref=dst, send_sem=send, recv_sem=recv, device_id=device, device_id_type=MESH
        )

    def halo_copy():
        return remote(series.at[0:8], halo, halo_s.at[0], halo_r.at[0], ((tm + 63) % 64, q))

    def z_copy(j):
        return remote(zall.at[0], zall.at[j], zs.at[j], zr.at[j], grp(j, 1))

    def seg_copy(s):
        return remote(segs.at[0], segs.at[s], ss.at[s], sr.at[s], col(s, 1))

    def part_copy(s):
        return remote(part.at[s], got.at[s], ps.at[s], pr.at[s], col(s, -1))

    def q_copy(j):
        return remote(qpart.at[j // 4], qgot.at[j], qs.at[j], qr.at[j], grp(j, -1))

    def final_copy(j):
        return remote(pall.at[0], pall.at[j], fs.at[j], fr.at[j], rep(j, 1))

    def each(low, high, do):
        lax.fori_loop(low, high, lambda i, c: (do(i), c)[1], 0)

    barrier = pltpu.get_barrier_semaphore()

    def hello(device):
        pl.semaphore_signal(barrier, inc=1, device_id=device, device_id_type=MESH)

    hello(((tm + 1) % 64, q))
    each(1, GROUP, lambda j: hello(grp(j, 1)))
    each(1, COLUMN, lambda s: hello(col(s, 1)))

    rows = queries[...]
    centered = rows - jnp.mean(rows, axis=1, keepdims=True)
    sigma = jnp.sqrt(jnp.mean(centered * centered, axis=1, keepdims=True) + 1e-05)
    zq = centered / sigma
    k = lax.broadcasted_iota(jnp.int32, (M, 384), 0)
    c = lax.broadcasted_iota(jnp.int32, (M, 384), 1)
    source = jnp.where(
        c < 128, 127 - c, jnp.where(c < 256, 383 - c, jnp.where(c < 352, 287 - c % REST, -1))
    )
    place = (k == source).astype(jnp.float32)
    zp = jnp.dot(zq, place, precision=lax.Precision.HIGHEST, preferred_element_type=jnp.float32)
    high, low = split(zp)
    kept = high.astype(jnp.float32) + low.astype(jnp.float32)
    lane = lax.broadcasted_iota(jnp.int32, (32, 384), 1)
    excess = jnp.sum(jnp.where(lane < M, kept, 0.0), axis=1, keepdims=True)
    zall[0] = jnp.where(lane < 352, zp, excess * (-1.0 / REST))
    acc[...] = jnp.full_like(acc, -1e30)
    ext[0:32] = series[...]

    pl.semaphore_wait(barrier, 1 + (GROUP - 1) + (COLUMN - 1))
    halo_copy().start()
    each(1, GROUP, lambda j: z_copy(j).start())
    halo_copy().wait_recv()
    ext[32:40] = jnp.where(tm == 63, tail[...], halo[...])

    x = ext[pl.ds(pl.multiple_of(q * 8, 8), 16)]
    segs[0, 0:16] = x - jnp.mean(x[0:8])
    for u, block in hankel(lambda i: segs[0, i : i + 1], 10):
        own_h[:, u * LANES : (u + 1) * LANES] = block
    for u in range(8):
        blocks = [own_h[:, (u + b) * LANES : (u + b + 1) * LANES] for b in (0, 1)]
        blocks.append(own_h[LANES - REST :, (u + 2) * LANES : (u + 3) * LANES])
        mean = sum(jnp.sum(b, axis=0, keepdims=True) for b in blocks) / M
        var = sum(jnp.sum((b - mean) * (b - mean), axis=0, keepdims=True) for b in blocks) / M
        segs[0, 16 + u : 17 + u] = 1.0 / jnp.sqrt(var + 1e-05)
    each(1, COLUMN, lambda s: seg_copy(s).start())

    def build(s, bh, bl, i):
        for u, block in hankel(lambda n: segs[s, n : n + 1], 10):
            bh[i, :, u * LANES : (u + 1) * LANES], bl[i, :, u * LANES : (u + 1) * LANES] = split(block)

    def compute(s, bh, bl, i):
        for t in range(SEG // 256):
            p = t * 256

            def two(ref):
                return [ref[i, :, p : p + 256], ref[i, :, p + 128 : p + 384]]

            def rest(ref):
                return ref[i, LANES - REST :, p + 256 : p + 512]

            h = jnp.concatenate(two(bh) + two(bh) + two(bl) + [rest(bh), rest(bh), rest(bl), rest(bh)], axis=0)
            out = jnp.dot(zcat[...], h, preferred_element_type=jnp.float32)
            best = jnp.max(out.reshape(32, 8, 256), axis=0)
            left = out[:, :LANES] * segs[s, 16 + 2 * t : 17 + 2 * t]
            right = out[:, LANES:] * segs[s, 17 + 2 * t : 18 + 2 * t]
            acc[...] = jnp.maximum(acc[...], jnp.maximum(left, right))
            part[s, 2 * t : 2 * t + 1] = jnp.max(best[:, :LANES], axis=0, keepdims=True)
            part[s, 2 * t + 1 : 2 * t + 2] = jnp.max(best[:, LANES:], axis=0, keepdims=True)

    build(0, bha, bla, 0)
    seg_copy(1).wait_recv()
    build(1, bha, bla, 1)

    each(1, GROUP, lambda j: z_copy(j).wait_recv())
    for j in range(GROUP):
        at = slice(32 * j, 32 * j + 32)
        value = zall[j]
        high, low = split(value)
        zcat[at, 0:256] = high[:, :256]
        zcat[at, 256:512] = low[:, :256]
        zcat[at, 512:768] = high[:, :256]
        four = lax.broadcasted_iota(jnp.int32, (32, LANES), 1)
        second = (four >= REST) & (four < 2 * REST)
        mixed = jnp.where(second, low[:, 256:].astype(jnp.float32), high[:, 256:].astype(jnp.float32))
        zcat[at, 768:896] = mixed.astype(jnp.bfloat16)

    def step(i, carry):
        s = 4 * i
        seg_copy(s + 2).wait_recv()
        seg_copy(s + 3).wait_recv()

        @pl.when(i < 7)
        def _():
            seg_copy(s + 4).wait_recv()
            seg_copy(s + 5).wait_recv()

        compute(s, bha, bla, 0)
        build(s + 2, bhb, blb, 0)
        compute(s + 1, bha, bla, 1)
        build(s + 3, bhb, blb, 1)
        compute(s + 2, bhb, blb, 0)
        build(jnp.minimum(s + 4, 30), bha, bla, 0)
        compute(s + 3, bhb, blb, 1)
        build(jnp.minimum(s + 5, 31), bha, bla, 1)

        @pl.when(i > 0)
        def _():
            part_copy(s).start()

        for n in (1, 2, 3):
            part_copy(s + n).start()
        return carry

    lax.fori_loop(0, COLUMN // 4, step, 0)

    best = jnp.max(jnp.transpose(acc[...]), axis=0, keepdims=True)
    qpart[0] = jnp.broadcast_to(best[:, :LANES], (8, LANES))
    qpart[1] = jnp.broadcast_to(best[:, LANES:], (8, LANES))
    each(1, GROUP, lambda j: q_copy(j).start())

    def distance(product):
        return jnp.sqrt(jnp.maximum(2.0 - 2.0 * product / M, 0.0))

    def fold(s, best):
        part_copy(s).wait_recv()
        return jnp.maximum(best, got[s])

    own = lax.fori_loop(1, COLUMN, fold, part[0])
    pall[0] = distance(own * segs[0, 16:24])
    each(1, REPLICAS, lambda j: final_copy(j).start())

    own = qpart[0, 0:1, 0:32]
    for j in range(1, GROUP):
        q_copy(j).wait_recv()
        own = jnp.maximum(own, qgot[j, 0:1, 32 * (j % 4) : 32 * (j % 4) + 32])
    qprof[...] = distance(own)

    for j in range(REPLICAS):
        if j:
            final_copy(j).wait_recv()
        at = pl.multiple_of(((q - j + 4) % 4) * 8, 8)
        prof[pl.ds(at, 8)] = pall[j]

    halo_copy().wait_send()
    each(1, GROUP, lambda j: z_copy(j).wait_send())
    each(1, COLUMN, lambda s: seg_copy(s).wait_send())
    each(1, COLUMN, lambda s: part_copy(s).wait_send())
    each(1, GROUP, lambda j: q_copy(j).wait_send())
    each(1, REPLICAS, lambda j: final_copy(j).wait_send())


def local(series, tail, queries):
    f32, bf16, dma = jnp.float32, jnp.bfloat16, pltpu.SemaphoreType.DMA
    vmem = pl.BlockSpec(memory_space=pltpu.VMEM)
    prof, qprof = pl.pallas_call(
        kernel,
        out_shape=[jax.ShapeDtypeStruct((32, LANES), f32), jax.ShapeDtypeStruct((1, 32), f32)],
        in_specs=[vmem] * 3,
        out_specs=[vmem] * 2,
        scratch_shapes=[
            pltpu.VMEM((40, LANES), f32),
            pltpu.VMEM((8, LANES), f32),
            pltpu.VMEM((LANES, 1280), f32),
            pltpu.VMEM((COLUMN, 24, LANES), f32),
            pltpu.VMEM((2, LANES, 1280), bf16),
            pltpu.VMEM((2, LANES, 1280), bf16),
            pltpu.VMEM((2, LANES, 1280), bf16),
            pltpu.VMEM((2, LANES, 1280), bf16),
            pltpu.VMEM((GROUP, 32, 384), f32),
            pltpu.VMEM((256, 896), bf16),
            pltpu.VMEM((256, LANES), f32),
            pltpu.VMEM((COLUMN, 8, LANES), f32),
            pltpu.VMEM((COLUMN, 8, LANES), f32),
            pltpu.VMEM((2, 8, LANES), f32),
            pltpu.VMEM((GROUP, 8, LANES), f32),
            pltpu.VMEM((REPLICAS, 8, LANES), f32),
            dma((1,)), dma((1,)),
            dma((GROUP,)), dma((GROUP,)),
            dma((COLUMN,)), dma((COLUMN,)),
            dma((COLUMN,)), dma((COLUMN,)),
            dma((GROUP,)), dma((GROUP,)),
            dma((REPLICAS,)), dma((REPLICAS,)),
        ],
        compiler_params=pltpu.CompilerParams(
            collective_id=0, has_side_effects=True, vmem_limit_bytes=40 * 2**20
        ),
    )(series.reshape(32, LANES), jnp.pad(tail, (0, 1024 - tail.shape[0])).reshape(8, LANES), queries)
    return prof.reshape(4096), qprof.reshape(32)


def solution(mesh):
    return jax.shard_map(
        local,
        mesh=mesh,
        in_specs=(P("tm"), P(), P(("tm", "query"), None)),
        out_specs=(P("tm"), P(("tm", "query"))),
        check_vma=False,
    )
```

```python
import jax
import jax.numpy as jnp
from jax import lax
from jax.experimental import pallas as pl
from jax.experimental.pallas import tpu as pltpu
from jax.sharding import PartitionSpec as P

M = 288
SEG = 1024
LANES = 128
COLUMN = 32
GROUP = 8
REPLICAS = 4
REST = M - 256
MESH = pl.DeviceIdType.MESH


def split(value):
    high = value.astype(jnp.bfloat16)
    low = (value - high.astype(jnp.float32)).astype(jnp.bfloat16)
    return high, low


def hankel(row, blocks):
    r = lax.broadcasted_iota(jnp.int32, (LANES, LANES), 0)
    lane = lax.broadcasted_iota(jnp.int32, (LANES, LANES), 1)
    this = pltpu.roll(jnp.broadcast_to(row(0), (LANES, LANES)), 1, 1, stride=1, stride_axis=0)
    for u in range(blocks):
        after = pltpu.roll(jnp.broadcast_to(row(u + 1), (LANES, LANES)), 1, 1, stride=1, stride_axis=0)
        yield u, jnp.where(lane <= r, this, after)
        this = after


def ahead(value, by):
    if by % LANES == 0:
        return pltpu.roll(value, 16 - by // LANES, 0)
    here = pltpu.roll(value, LANES - by, 1)
    lanes = lax.broadcasted_iota(jnp.int32, (16, LANES), 1)
    return jnp.where(lanes < LANES - by, here, pltpu.roll(here, 15, 0))


def scales(x):
    mean, dev, n = x, None, 1
    while n < 256:
        gap = ahead(mean, n) - mean
        joined = gap * gap * (n / 2)
        dev = joined if dev is None else dev + ahead(dev, n) + joined
        mean = mean + 0.5 * gap
        n *= 2
        if n == REST:
            mean_rest, dev_rest = mean, dev
    gap = ahead(mean_rest, 256) - mean
    dev = dev + ahead(dev_rest, 256) + gap * gap * (256 * REST / M)
    return 1.0 / jnp.sqrt(dev[0:8] / M + 1e-05)


def kernel(
    series, tail, queries, prof, qprof,
    ext, tail_v, rows_v, segs, bha, bla, bhb, blb, zall, zcat, acc, part, got, found, qpart, qgot, pall, last,
    ls, halo_s, halo_r, zs, zr, ss, sr, ps, pr, qs, qr, fs, fr,
):
    tm, q = lax.axis_index("tm"), lax.axis_index("query")
    zz, yy, xh = lax.div(tm, 8), lax.rem(lax.div(tm, 2), 4), lax.rem(tm, 2)
    xx, core = xh * 2 + lax.div(q, 2), lax.rem(q, 2)

    def col(s, sign):
        s = jnp.int32(s)
        z2 = lax.rem(zz + sign * lax.div(s, 4) + 8, 8)
        y2 = lax.rem(yy + sign * lax.rem(s, 4) + 4, 4)
        return (z2 * 8 + y2 * 2 + xh, q)

    def grp(j, sign):
        x2 = lax.rem(xx + sign * lax.div(j, 2) + 4, 4)
        c2 = lax.rem(core + lax.rem(j, 2), 2)
        return (tm - xh + lax.div(x2, 2), lax.rem(x2, 2) * 2 + c2)

    def rep(j, sign):
        return (tm, lax.rem(q + sign * j + 4, 4))

    def remote(src, dst, send, recv, device):
        return pltpu.make_async_remote_copy(
            src_ref=src, dst_ref=dst, send_sem=send, recv_sem=recv, device_id=device, device_id_type=MESH
        )

    def halo_copy():
        return remote(ext.at[0:8], ext.at[32:40], halo_s.at[0], halo_r.at[0], (lax.rem(tm + 63, 64), 3))

    def z_copy(j):
        return remote(zall.at[0], zall.at[j], zs.at[j], zr.at[j], grp(jnp.int32(j), 1))

    def z_forward(j):
        return remote(zall.at[j - 1], zall.at[j], zs.at[j], zr.at[j], grp(jnp.int32(1), 1))

    def seg_copy(s):
        return remote(segs.at[0], segs.at[s], ss.at[s], sr.at[s], col(s, 1))

    def part_copy(s):
        return remote(part.at[s], got.at[s], ps.at[s], pr.at[s], col(s, -1))

    def q_copy(j):
        return remote(qpart.at[j % 2], qgot.at[j], qs.at[j], qr.at[j], grp(jnp.int32(j), -1))

    def last_copy(n, j):
        device = (col(28 + n, -1)[0], lax.rem(q + j, 4))
        return remote(part.at[28 + n], last.at[4 * j + n], fs.at[4 * j + n], fr.at[4 * j + n], device)

    def final_copy(j):
        return remote(pall.at[0], pall.at[j], fs.at[16 + j], fr.at[16 + j], rep(jnp.int32(j), 1))

    def each(low, high, do):
        lax.fori_loop(low, high, lambda i, c: (do(i), c)[1], 0)

    loads = [
        pltpu.make_async_copy(queries, rows_v, ls.at[0]),
        pltpu.make_async_copy(series, ext.at[0:32], ls.at[1]),
        pltpu.make_async_copy(tail, tail_v, ls.at[2]),
    ]
    for load in loads:
        load.start()

    barrier = pltpu.get_barrier_semaphore()

    def hello(device):
        pl.semaphore_signal(barrier, inc=1, device_id=device, device_id_type=MESH)

    each(1, GROUP, lambda j: hello(grp(j, 1)))
    each(1, COLUMN, lambda s: hello(col(s, 1)))
    hello((lax.rem(tm + 1, 64), lax.rem(q + 2, 4)))
    each(0, 12, lambda i: hello((col(28 + lax.rem(i, 4), 1)[0], lax.rem(q + 1 + lax.div(i, 4), 4))))

    loads[0].wait()
    rows = rows_v[...]
    centered = rows - jnp.mean(rows, axis=1, keepdims=True)
    sigma = jnp.sqrt(jnp.mean(centered * centered, axis=1, keepdims=True) + 1e-05)
    zq = centered / sigma
    k = lax.broadcasted_iota(jnp.int32, (M, 384), 0)
    c = lax.broadcasted_iota(jnp.int32, (M, 384), 1)
    source = jnp.where(c < 128, 127 - c, jnp.where(c < 256, 383 - c, 287 - c % REST))
    place = (k == source).astype(jnp.float32)
    zp = jnp.dot(zq, place, precision=lax.Precision.HIGHEST, preferred_element_type=jnp.float32)
    lane = lax.broadcasted_iota(jnp.int32, (8, LANES), 1)
    quad = lane // REST
    packed = zp[24:32, 256:384]
    for g in range(3):
        packed = jnp.where(quad == g, zp[8 * g : 8 * g + 8, 256:384], packed)
    zall[0, 0:32] = zp[:, :128]
    zall[0, 32:64] = zp[:, 128:256]
    zall[0, 64:72] = packed
    acc[...] = jnp.full_like(acc, -1e30)
    loads[1].wait()
    loads[2].wait()

    @pl.when((q == 3) & (tm == 63))
    def _():
        ext[32:40] = jnp.zeros((8, LANES), jnp.float32)
        ext[32:33] = tail_v[0:128].reshape(1, LANES)
        ext[33:34] = tail_v[128:256].reshape(1, LANES)
        ext[34:35, 0 : REST - 1] = tail_v[256 : M - 1].reshape(1, REST - 1)

    def message():
        x = ext[pl.ds(pl.multiple_of(q * 8, 8), 16)]
        x = x - jnp.mean(x[0:8])
        segs[0, 0:16] = x
        segs[0, 16:24] = scales(x)

    @pl.when((q < 3) | (tm == 63))
    def _():
        message()

    pl.semaphore_wait(barrier, 1 + (GROUP - 1) + (COLUMN - 1) + 12)

    @pl.when((q == 1) & (tm > 0))
    def _():
        halo_copy().start()

    for j in (2, 6, 4, 1):
        z_copy(j).start()

    @pl.when((q == 3) & (tm < 63))
    def _():
        halo_copy().wait_recv()
        message()

    each(1, COLUMN, lambda s: seg_copy(s).start())

    def build(s, bh, bl, i):
        for u, block in hankel(lambda n: segs[s, n : n + 1], 10):
            bh[i, :, u * LANES : (u + 1) * LANES], bl[i, :, u * LANES : (u + 1) * LANES] = split(block)

    def compute(s, bh, bl, i, low=0, high=256):
        for t in range(SEG // 256):
            p = t * 256

            def two(ref):
                return [ref[i, :, p : p + 256], ref[i, :, p + 128 : p + 384]]

            def rest(ref):
                return ref[i, LANES - REST :, p + 256 : p + 512]

            h = jnp.concatenate(two(bh) + two(bh) + two(bl) + [rest(bh), rest(bh), rest(bl), rest(bh)], axis=0)
            out = jnp.dot(zcat[low:high], h, preferred_element_type=jnp.float32)
            best = jnp.max(out.reshape((high - low) // 8, 8, 256), axis=0)
            scaled = []
            for n in (0, 1):
                u, half = 2 * t + n, slice(n * LANES, (n + 1) * LANES)
                scale = segs[s, 16 + u : 17 + u]
                scaled.append(out[:, half] * scale)
                top = jnp.max(best[:, half], axis=0, keepdims=True) * scale
                part[s, u : u + 1] = jnp.maximum(part[s, u : u + 1], top) if low else top
            acc[low:high] = jnp.maximum(acc[low:high], jnp.maximum(*scaled))

    def take(j):
        at = slice(32 * (j // 2) + 128 * (j % 2), 32 * (j // 2) + 128 * (j % 2) + 32)
        total = jnp.zeros((32, 1), jnp.float32)
        for b in (0, 1):
            value = zall[j, 32 * b : 32 * b + 32]
            high, low = split(value)
            zcat[at, 128 * b : 128 * b + 128] = high
            zcat[at, 256 + 128 * b : 384 + 128 * b] = low
            zcat[at, 512 + 128 * b : 640 + 128 * b] = high
            total += jnp.sum(high.astype(jnp.float32) + low.astype(jnp.float32), axis=1, keepdims=True)
        four = []
        for g in range(4):
            value = jnp.where(quad == g, zall[j, 64:72], 0.0)
            value = value + pltpu.roll(value, 32, 1)
            four.append(value + pltpu.roll(value, 64, 1))
        value = jnp.concatenate(four, axis=0)
        high, low = split(value)
        high, low = high.astype(jnp.float32), low.astype(jnp.float32)
        lanes = lax.broadcasted_iota(jnp.int32, (32, LANES), 1)
        total += jnp.sum(jnp.where(lanes < REST, high + low, 0.0), axis=1, keepdims=True)
        part_of = lanes // REST
        mixed = jnp.where(part_of == 1, low, jnp.where(part_of == 3, total * (-1.0 / REST), high))
        zcat[at, 768:896] = mixed.astype(jnp.bfloat16)

    def four(s, last=False):
        for n in (2, 3) if last else (2, 3, 4, 5):
            seg_copy(s + n).wait_recv()
        compute(s, bha, bla, 0)
        build(s + 2, bhb, blb, 0)
        compute(s + 1, bha, bla, 1)
        build(s + 3, bhb, blb, 1)
        compute(s + 2, bhb, blb, 0)
        if not last:
            build(s + 4, bha, bla, 0)
        compute(s + 3, bhb, blb, 1)
        if not last:
            build(s + 5, bha, bla, 1)
        for n in range(4):
            if last:
                for j in range(REPLICAS):
                    last_copy(n, j).start()
            else:
                part_copy(s + n).start()

    def fold(s):
        part_copy(s).wait_recv()
        found[...] = jnp.maximum(found[...], got[s])

    take(0)
    build(0, bha, bla, 0)
    for j in (2, 6, 4):
        z_copy(j).wait_recv()
        z_forward(j + 1).start()
        take(j)
    compute(0, bha, bla, 0, 0, 128)
    seg_copy(1).wait_recv()
    build(1, bha, bla, 1)
    compute(1, bha, bla, 1, 0, 128)
    z_copy(1).wait_recv()
    take(1)
    for j in (3, 7, 5):
        z_forward(j).wait_recv()
        take(j)
    for n in (2, 3, 4, 5):
        seg_copy(n).wait_recv()
    compute(0, bha, bla, 0, 128, 256)
    build(2, bhb, blb, 0)
    compute(1, bha, bla, 1, 128, 256)
    build(3, bhb, blb, 1)
    compute(2, bhb, blb, 0)
    build(4, bha, bla, 0)
    compute(3, bhb, blb, 1)
    build(5, bha, bla, 1)
    for n in (1, 2, 3):
        part_copy(n).start()
    found[...] = part[0]

    def step(i, carry):
        s = 8 * i + 4
        four(s)
        four(s + 4)

        return carry

    lax.fori_loop(0, 3, step, 0)
    four(28, last=True)

    best = jnp.max(jnp.transpose(acc[...]), axis=0, keepdims=True)
    qpart[0] = jnp.broadcast_to(best[:, :LANES], (8, LANES))
    qpart[1] = jnp.broadcast_to(best[:, LANES:], (8, LANES))
    for j in range(1, GROUP):
        q_copy(j).start()

    def distance(product):
        return jnp.sqrt(jnp.maximum(2.0 - 2.0 * product / M, 0.0))

    for n in range(1, 28):
        fold(n)
    pall[0] = found[...]
    for j in range(1, REPLICAS):
        final_copy(j).start()

    own = qpart[0, 0:1, 0:32]
    for j in range(1, GROUP):
        q_copy(j).wait_recv()
        own = jnp.maximum(own, qgot[j, 0:1, 32 * (j // 2) : 32 * (j // 2) + 32])
    qprof[...] = distance(own)

    for j in range(REPLICAS):
        for n in range(4):
            last_copy(n, j).wait_recv()
        if j:
            final_copy(j).wait_recv()
        best = jnp.maximum(pall[j], jnp.max(last[4 * j : 4 * j + 4], axis=0))
        at = pl.multiple_of(lax.rem(q - j + 4, 4) * 8, 8)
        prof[pl.ds(at, 8)] = distance(best)

    @pl.when((q == 1) & (tm > 0))
    def _():
        halo_copy().wait_send()

    for j in range(1, GROUP):
        (z_forward(j) if j in (3, 5, 7) else z_copy(j)).wait_send()
        q_copy(j).wait_send()
    for j in range(1, REPLICAS):
        final_copy(j).wait_send()
    for n in range(1, COLUMN):
        seg_copy(n).wait_send()
    for n in range(1, 28):
        part_copy(n).wait_send()
    for n in range(4):
        for j in range(REPLICAS):
            last_copy(n, j).wait_send()


def local(series, tail, queries):
    f32, bf16, dma = jnp.float32, jnp.bfloat16, pltpu.SemaphoreType.DMA
    vmem = pl.BlockSpec(memory_space=pltpu.VMEM)
    prof, qprof = pl.pallas_call(
        kernel,
        out_shape=[jax.ShapeDtypeStruct((32, LANES), f32), jax.ShapeDtypeStruct((1, 32), f32)],
        in_specs=[pl.BlockSpec(memory_space=pl.ANY)] * 3,
        out_specs=[vmem] * 2,
        scratch_shapes=[
            pltpu.VMEM((40, LANES), f32),
            pltpu.VMEM((M - 1,), f32),
            pltpu.VMEM((32, M), f32),
            pltpu.VMEM((COLUMN, 24, LANES), f32),
            pltpu.VMEM((2, LANES, 1280), bf16),
            pltpu.VMEM((2, LANES, 1280), bf16),
            pltpu.VMEM((2, LANES, 1280), bf16),
            pltpu.VMEM((2, LANES, 1280), bf16),
            pltpu.VMEM((GROUP, 72, LANES), f32),
            pltpu.VMEM((256, 896), bf16),
            pltpu.VMEM((256, LANES), f32),
            pltpu.VMEM((COLUMN, 8, LANES), f32),
            pltpu.VMEM((COLUMN, 8, LANES), f32),
            pltpu.VMEM((8, LANES), f32),
            pltpu.VMEM((2, 8, LANES), f32),
            pltpu.VMEM((GROUP, 8, LANES), f32),
            pltpu.VMEM((REPLICAS, 8, LANES), f32),
            pltpu.VMEM((4 * REPLICAS, 8, LANES), f32),
            dma((3,)), dma((1,)), dma((1,)),
            dma((GROUP,)), dma((GROUP,)),
            dma((COLUMN,)), dma((COLUMN,)),
            dma((COLUMN,)), dma((COLUMN,)),
            dma((GROUP,)), dma((GROUP,)),
            dma((20,)), dma((20,)),
        ],
        compiler_params=pltpu.CompilerParams(
            collective_id=0, has_side_effects=True, vmem_limit_bytes=60 * 2**20
        ),
    )(series.reshape(32, LANES), tail, queries)
    return prof.reshape(4096), qprof.reshape(32)


def solution(mesh):
    return jax.shard_map(
        local,
        mesh=mesh,
        in_specs=(P("tm"), P(), P(("tm", "query"), None)),
        out_specs=(P("tm"), P(("tm", "query"))),
        check_vma=False,
    )
```

```python
import jax
import jax.numpy as jnp
from jax import lax
from jax.experimental import pallas as pl
from jax.experimental.pallas import tpu as pltpu
from jax.sharding import PartitionSpec as P

M = 288
SEG = 1024
LANES = 128
COLUMN = 32
GROUP = 8
REPLICAS = 4
REST = M - 256
MESH = pl.DeviceIdType.MESH


def split(value):
    high = value.astype(jnp.bfloat16)
    low = (value - high.astype(jnp.float32)).astype(jnp.bfloat16)
    return high, low


def hankel(row, blocks):
    r = lax.broadcasted_iota(jnp.int32, (LANES, LANES), 0)
    lane = lax.broadcasted_iota(jnp.int32, (LANES, LANES), 1)
    this = pltpu.roll(jnp.broadcast_to(row(0), (LANES, LANES)), 1, 1, stride=1, stride_axis=0)
    for u in range(blocks):
        after = pltpu.roll(jnp.broadcast_to(row(u + 1), (LANES, LANES)), 1, 1, stride=1, stride_axis=0)
        yield u, jnp.where(lane <= r, this, after)
        this = after


def ahead(value, by):
    if by % LANES == 0:
        return pltpu.roll(value, 16 - by // LANES, 0)
    here = pltpu.roll(value, LANES - by, 1)
    lanes = lax.broadcasted_iota(jnp.int32, (16, LANES), 1)
    return jnp.where(lanes < LANES - by, here, pltpu.roll(here, 15, 0))


def scales(x):
    mean, dev, n = x, None, 1
    while n < 256:
        gap = ahead(mean, n) - mean
        joined = gap * gap * (n / 2)
        dev = joined if dev is None else dev + ahead(dev, n) + joined
        mean = mean + 0.5 * gap
        n *= 2
        if n == REST:
            mean_rest, dev_rest = mean, dev
    gap = ahead(mean_rest, 256) - mean
    dev = dev + ahead(dev_rest, 256) + gap * gap * (256 * REST / M)
    return 1.0 / jnp.sqrt(dev[0:8] / M + 1e-05)


def kernel(
    series, tail, queries, prof, qprof,
    ext, tail_v, rows_v, segs, bha, bla, bhb, blb, zall, zcat, acc, part, got, found, qpart, qgot, pall, last,
    ls, halo_s, halo_r, zs, zr, ss, sr, ps, pr, qs, qr, fs, fr,
):
    tm, q = lax.axis_index("tm"), lax.axis_index("query")
    zz, yy, xh = lax.div(tm, 8), lax.rem(lax.div(tm, 2), 4), lax.rem(tm, 2)
    xx, core = xh * 2 + lax.div(q, 2), lax.rem(q, 2)

    z_at = [lax.rem(zz + n, 8) * 8 for n in range(8)]
    y_at = [lax.rem(yy + n, 4) * 2 + xh for n in range(4)]
    x_at = [lax.rem(xx + n, 4) for n in range(4)]
    g_at = [tm - xh + lax.div(x, 2) for x in x_at]
    q_at = [[lax.rem(x, 2) * 2 + c for c in (core, 1 - core)] for x in x_at]
    r_at = [lax.rem(q + n, 4) for n in range(4)]

    def col(s, sign):
        return (z_at[sign * (s // 4) % 8] + y_at[sign * (s % 4) % 4], q)

    def place(b, n):
        return (lax.rem(zz - b + 8, 8) * 8 + y_at[-n % 4], q)

    def grp(j, sign):
        return (g_at[sign * (j // 2) % 4], q_at[sign * (j // 2) % 4][j % 2])

    def rep(j, sign):
        return (tm, r_at[sign * j % 4])

    def remote(src, dst, send, recv, device):
        return pltpu.make_async_remote_copy(
            src_ref=src, dst_ref=dst, send_sem=send, recv_sem=recv, device_id=device, device_id_type=MESH
        )

    def halo_copy():
        return remote(ext.at[0:8], ext.at[32:40], halo_s.at[0], halo_r.at[0], (lax.rem(tm + 63, 64), 3))

    def z_copy(j):
        return remote(zall.at[0], zall.at[j], zs.at[j], zr.at[j], grp(j, 1))

    def z_forward(j):
        return remote(zall.at[j - 1], zall.at[j], zs.at[j], zr.at[j], grp(1, 1))

    def seg_copy(s):
        device = col(s, 1) if isinstance(s, int) else (tm, q)
        return remote(segs.at[0], segs.at[s], ss.at[s], sr.at[s], device)

    def part_copy(s, device=None):
        return remote(part.at[s], got.at[s], ps.at[s], pr.at[s], device or col(s, -1))

    def q_copy(j):
        return remote(qpart.at[j % 2], qgot.at[j], qs.at[j], qr.at[j], grp(j, -1))

    def last_copy(n, j):
        device = (col(28 + n, -1)[0], r_at[j])
        return remote(part.at[28 + n], last.at[4 * j + n], fs.at[4 * j + n], fr.at[4 * j + n], device)

    def final_copy(j):
        return remote(pall.at[0], pall.at[j], fs.at[16 + j], fr.at[16 + j], rep(j, 1))

    def each(low, high, do):
        lax.fori_loop(low, high, lambda i, c: (do(i), c)[1], 0)

    loads = [
        pltpu.make_async_copy(queries, rows_v, ls.at[0]),
        pltpu.make_async_copy(series, ext.at[0:32], ls.at[1]),
        pltpu.make_async_copy(tail, tail_v, ls.at[2]),
    ]
    for load in loads:
        load.start()

    barrier = pltpu.get_barrier_semaphore()

    def hello(device):
        pl.semaphore_signal(barrier, inc=1, device_id=device, device_id_type=MESH)

    for j in range(1, GROUP):
        hello(grp(j, 1))
    for s in range(1, COLUMN):
        hello(col(s, 1))
    hello((lax.rem(tm + 1, 64), r_at[2]))
    for j in range(1, REPLICAS):
        for n in range(4):
            hello((col(28 + n, 1)[0], r_at[j]))

    loads[0].wait()
    rows = rows_v[...]
    centered = rows - jnp.mean(rows, axis=1, keepdims=True)
    sigma = jnp.sqrt(jnp.mean(centered * centered, axis=1, keepdims=True) + 1e-05)
    zq = centered / sigma
    k = lax.broadcasted_iota(jnp.int32, (M, 384), 0)
    c = lax.broadcasted_iota(jnp.int32, (M, 384), 1)
    source = jnp.where(c < 128, 127 - c, jnp.where(c < 256, 383 - c, 287 - c % REST))
    order = (k == source).astype(jnp.bfloat16)
    zp = sum(jnp.dot(piece, order, preferred_element_type=jnp.float32) for piece in split(zq))
    lane = lax.broadcasted_iota(jnp.int32, (8, LANES), 1)
    quad = lane // REST
    packed = zp[24:32, 256:384]
    for g in range(3):
        packed = jnp.where(quad == g, zp[8 * g : 8 * g + 8, 256:384], packed)
    zall[0, 0:32] = zp[:, :128]
    zall[0, 32:64] = zp[:, 128:256]
    zall[0, 64:72] = packed
    loads[1].wait()
    loads[2].wait()

    @pl.when((q == 3) & (tm == 63))
    def _():
        ext[32:40] = jnp.zeros((8, LANES), jnp.float32)
        ext[32:33] = tail_v[0:128].reshape(1, LANES)
        ext[33:34] = tail_v[128:256].reshape(1, LANES)
        ext[34:35, 0 : REST - 1] = tail_v[256 : M - 1].reshape(1, REST - 1)

    def message():
        x = ext[pl.ds(pl.multiple_of(q * 8, 8), 16)]
        x = x - jnp.mean(x[0:8])
        segs[0, 0:16] = x
        segs[0, 16:24] = scales(x)

    @pl.when((q < 3) | (tm == 63))
    def _():
        message()

    pl.semaphore_wait(barrier, 1 + (GROUP - 1) + (COLUMN - 1) + 12)

    @pl.when((q == 1) & (tm > 0))
    def _():
        halo_copy().start()

    for j in (2, 6, 4, 1):
        z_copy(j).start()

    @pl.when((q == 3) & (tm < 63))
    def _():
        halo_copy().wait_recv()

    @pl.when((q == 3) & (tm < 63))
    def _():
        message()
    for s in range(1, COLUMN):
        seg_copy(s).start()
    acc[...] = jnp.full_like(acc, -1e30)

    def build(s, bh, bl, i):
        for u, block in hankel(lambda n: segs[s, n : n + 1], 10):
            bh[i, :, u * LANES : (u + 1) * LANES], bl[i, :, u * LANES : (u + 1) * LANES] = split(block)

    def compute(s, bh, bl, i, low=0, high=256):
        for t in range(SEG // 256):
            p = t * 256

            def two(ref):
                return [ref[i, :, p : p + 256], ref[i, :, p + 128 : p + 384]]

            def rest(ref):
                return ref[i, LANES - REST :, p + 256 : p + 512]

            h = jnp.concatenate(two(bh) + two(bh) + two(bl) + [rest(bh), rest(bh), rest(bl), rest(bh)], axis=0)
            out = jnp.dot(zcat[low:high], h, preferred_element_type=jnp.float32)
            best = jnp.max(out.reshape((high - low) // 8, 8, 256), axis=0)
            scaled = []
            for n in (0, 1):
                u, half = 2 * t + n, slice(n * LANES, (n + 1) * LANES)
                scale = segs[s, 16 + u : 17 + u]
                scaled.append(out[:, half] * scale)
                top = jnp.max(best[:, half], axis=0, keepdims=True) * scale
                part[s, u : u + 1] = jnp.maximum(part[s, u : u + 1], top) if low else top
            acc[low:high] = jnp.maximum(acc[low:high], jnp.maximum(*scaled))

    def take(j):
        at = slice(32 * (j // 2) + 128 * (j % 2), 32 * (j // 2) + 128 * (j % 2) + 32)
        total = jnp.zeros((32, 1), jnp.float32)
        for b in (0, 1):
            value = zall[j, 32 * b : 32 * b + 32]
            high, low = split(value)
            zcat[at, 128 * b : 128 * b + 128] = high
            zcat[at, 256 + 128 * b : 384 + 128 * b] = low
            zcat[at, 512 + 128 * b : 640 + 128 * b] = high
            total += jnp.sum(high.astype(jnp.float32) + low.astype(jnp.float32), axis=1, keepdims=True)
        four = []
        for g in range(4):
            value = jnp.where(quad == g, zall[j, 64:72], 0.0)
            value = value + pltpu.roll(value, 32, 1)
            four.append(value + pltpu.roll(value, 64, 1))
        value = jnp.concatenate(four, axis=0)
        high, low = split(value)
        high, low = high.astype(jnp.float32), low.astype(jnp.float32)
        lanes = lax.broadcasted_iota(jnp.int32, (32, LANES), 1)
        total += jnp.sum(jnp.where(lanes < REST, high + low, 0.0), axis=1, keepdims=True)
        part_of = lanes // REST
        mixed = jnp.where(part_of == 1, low, jnp.where(part_of == 3, total * (-1.0 / REST), high))
        zcat[at, 768:896] = mixed.astype(jnp.bfloat16)

    def four(s, last=False):
        compute(s, bha, bla, 0)
        build(s + 2, bhb, blb, 0)
        compute(s + 1, bha, bla, 1)
        build(s + 3, bhb, blb, 1)
        compute(s + 2, bhb, blb, 0)
        if not last:
            build(s + 4, bha, bla, 0)
        compute(s + 3, bhb, blb, 1)
        if not last:
            build(s + 5, bha, bla, 1)

    def fold(s):
        part_copy(s).wait_recv()
        found[...] = jnp.maximum(found[...], got[s])

    take(0)
    build(0, bha, bla, 0)
    for j in (2, 6, 4):
        z_copy(j).wait_recv()
        z_forward(j + 1).start()
        take(j)
    compute(0, bha, bla, 0, 0, 128)
    seg_copy(1).wait_recv()
    build(1, bha, bla, 1)
    compute(1, bha, bla, 1, 0, 128)
    z_copy(1).wait_recv()
    take(1)
    for j in (3, 7, 5):
        z_forward(j).wait_recv()
        take(j)
    for n in (2, 3, 4, 5):
        seg_copy(n).wait_recv()
    compute(0, bha, bla, 0, 128, 256)
    build(2, bhb, blb, 0)
    compute(1, bha, bla, 1, 128, 256)
    build(3, bhb, blb, 1)
    compute(2, bhb, blb, 0)
    build(4, bha, bla, 0)
    compute(3, bhb, blb, 1)
    build(5, bha, bla, 1)
    for n in (1, 2, 3):
        part_copy(n).start()
    found[...] = part[0]

    def step(i, carry):
        s = 8 * i + 4
        for h in (0, 4):
            for n in range(2, 6):
                seg_copy(s + h + n).wait_recv()
            four(s + h)
            for n in range(4):
                part_copy(s + h + n, place(2 * i + 1 + h // 4, n)).start()
        return carry

    lax.fori_loop(0, 3, step, 0)
    for n in (30, 31):
        seg_copy(n).wait_recv()
    four(28, last=True)
    for n in range(4):
        for j in range(REPLICAS):
            last_copy(n, j).start()

    best = jnp.max(jnp.transpose(acc[...]), axis=0, keepdims=True)
    qpart[0] = jnp.broadcast_to(best[:, :LANES], (8, LANES))
    qpart[1] = jnp.broadcast_to(best[:, LANES:], (8, LANES))
    for j in range(1, GROUP):
        q_copy(j).start()

    def distance(product):
        return jnp.sqrt(jnp.maximum(2.0 - 2.0 * product / M, 0.0))

    for n in range(1, 28):
        fold(n)
    pall[0] = found[...]
    for j in range(1, REPLICAS):
        final_copy(j).start()

    own = qpart[0, 0:1, 0:32]
    for j in range(1, GROUP):
        q_copy(j).wait_recv()
        own = jnp.maximum(own, qgot[j, 0:1, 32 * (j // 2) : 32 * (j // 2) + 32])
    qprof[...] = distance(own)

    for j in range(REPLICAS):
        for n in range(4):
            last_copy(n, j).wait_recv()
        if j:
            final_copy(j).wait_recv()
        best = jnp.maximum(pall[j], jnp.max(last[4 * j : 4 * j + 4], axis=0))
        at = pl.multiple_of(lax.rem(q - j + 4, 4) * 8, 8)
        prof[pl.ds(at, 8)] = distance(best)

    @pl.when((q == 1) & (tm > 0))
    def _():
        halo_copy().wait_send()

    for j in range(1, GROUP):
        (z_forward(j) if j in (3, 5, 7) else z_copy(j)).wait_send()
        q_copy(j).wait_send()
    for j in range(1, REPLICAS):
        final_copy(j).wait_send()
    for n in range(1, COLUMN):
        seg_copy(n).wait_send()
    for n in range(1, 28):
        part_copy(n).wait_send()
    for n in range(4):
        for j in range(REPLICAS):
            last_copy(n, j).wait_send()


def local(series, tail, queries):
    f32, bf16, dma = jnp.float32, jnp.bfloat16, pltpu.SemaphoreType.DMA
    vmem = pl.BlockSpec(memory_space=pltpu.VMEM)
    prof, qprof = pl.pallas_call(
        kernel,
        out_shape=[jax.ShapeDtypeStruct((32, LANES), f32), jax.ShapeDtypeStruct((1, 32), f32)],
        in_specs=[pl.BlockSpec(memory_space=pl.ANY)] * 3,
        out_specs=[vmem] * 2,
        scratch_shapes=[
            pltpu.VMEM((40, LANES), f32),
            pltpu.VMEM((M - 1,), f32),
            pltpu.VMEM((32, M), f32),
            pltpu.VMEM((COLUMN, 24, LANES), f32),
            pltpu.VMEM((2, LANES, 1280), bf16),
            pltpu.VMEM((2, LANES, 1280), bf16),
            pltpu.VMEM((2, LANES, 1280), bf16),
            pltpu.VMEM((2, LANES, 1280), bf16),
            pltpu.VMEM((GROUP, 72, LANES), f32),
            pltpu.VMEM((256, 896), bf16),
            pltpu.VMEM((256, LANES), f32),
            pltpu.VMEM((COLUMN, 8, LANES), f32),
            pltpu.VMEM((COLUMN, 8, LANES), f32),
            pltpu.VMEM((8, LANES), f32),
            pltpu.VMEM((2, 8, LANES), f32),
            pltpu.VMEM((GROUP, 8, LANES), f32),
            pltpu.VMEM((REPLICAS, 8, LANES), f32),
            pltpu.VMEM((4 * REPLICAS, 8, LANES), f32),
            dma((3,)), dma((1,)), dma((1,)),
            dma((GROUP,)), dma((GROUP,)),
            dma((COLUMN,)), dma((COLUMN,)),
            dma((COLUMN,)), dma((COLUMN,)),
            dma((GROUP,)), dma((GROUP,)),
            dma((20,)), dma((20,)),
        ],
        compiler_params=pltpu.CompilerParams(
            collective_id=0, has_side_effects=True, vmem_limit_bytes=60 * 2**20
        ),
    )(series.reshape(32, LANES), tail, queries)
    return prof.reshape(4096), qprof.reshape(32)


def solution(mesh):
    return jax.shard_map(
        local,
        mesh=mesh,
        in_specs=(P("tm"), P(), P(("tm", "query"), None)),
        out_specs=(P("tm"), P(("tm", "query"))),
        check_vma=False,
    )
```

```python
import jax
import jax.numpy as jnp
from jax import lax
from jax.experimental import pallas as pl
from jax.experimental.pallas import tpu as pltpu
from jax.sharding import PartitionSpec as P

M = 288
SEG = 1024
LANES = 128
COLUMN = 32
GROUP = 8
REPLICAS = 4
REST = M - 256
MESH = pl.DeviceIdType.MESH


def split(value):
    high = value.astype(jnp.bfloat16)
    low = (value - high.astype(jnp.float32)).astype(jnp.bfloat16)
    return high, low


def hankel(row, blocks):
    r = lax.broadcasted_iota(jnp.int32, (LANES, LANES), 0)
    lane = lax.broadcasted_iota(jnp.int32, (LANES, LANES), 1)
    this = pltpu.roll(jnp.broadcast_to(row(0), (LANES, LANES)), 1, 1, stride=1, stride_axis=0)
    for u in range(blocks):
        after = pltpu.roll(jnp.broadcast_to(row(u + 1), (LANES, LANES)), 1, 1, stride=1, stride_axis=0)
        yield u, jnp.where(lane <= r, this, after)
        this = after


def ahead(value, by):
    if by % LANES == 0:
        return pltpu.roll(value, 16 - by // LANES, 0)
    here = pltpu.roll(value, LANES - by, 1)
    lanes = lax.broadcasted_iota(jnp.int32, (16, LANES), 1)
    return jnp.where(lanes < LANES - by, here, pltpu.roll(here, 15, 0))


def scales(x):
    mean, dev, n = x, None, 1
    while n < 256:
        gap = ahead(mean, n) - mean
        joined = gap * gap * (n / 2)
        dev = joined if dev is None else dev + ahead(dev, n) + joined
        mean = mean + 0.5 * gap
        n *= 2
        if n == REST:
            mean_rest, dev_rest = mean, dev
    gap = ahead(mean_rest, 256) - mean
    dev = dev + ahead(dev_rest, 256) + gap * gap * (256 * REST / M)
    return 1.0 / jnp.sqrt(dev[0:8] / M + 1e-05)


def kernel(
    series, tail, queries, prof, qprof,
    ext, tail_v, rows_v, segs, bha, bla, bhb, blb, zall, zcat, acc, part, got, found, qpart, qgot, pall, last,
    ls, halo_s, halo_r, zs, zr, ss, sr, ps, pr, qs, qr, fs, fr,
):
    tm, q = lax.axis_index("tm"), lax.axis_index("query")
    zz, yy, xh = lax.div(tm, 8), lax.rem(lax.div(tm, 2), 4), lax.rem(tm, 2)
    xx, core = xh * 2 + lax.div(q, 2), lax.rem(q, 2)

    z_at = [lax.rem(zz + n, 8) * 8 for n in range(8)]
    y_at = [lax.rem(yy + n, 4) * 2 + xh for n in range(4)]
    x_at = [lax.rem(xx + n, 4) for n in range(4)]
    g_at = [tm - xh + lax.div(x, 2) for x in x_at]
    q_at = [[lax.rem(x, 2) * 2 + c for c in (core, 1 - core)] for x in x_at]
    r_at = [lax.rem(q + n, 4) for n in range(4)]

    def col(s, sign):
        return (z_at[sign * (s // 4) % 8] + y_at[sign * (s % 4) % 4], q)

    def place(b, n):
        return (lax.rem(zz - b + 8, 8) * 8 + y_at[-n % 4], q)

    def grp(j, sign):
        return (g_at[sign * (j // 2) % 4], q_at[sign * (j // 2) % 4][j % 2])

    def rep(j, sign):
        return (tm, r_at[sign * j % 4])

    def remote(src, dst, send, recv, device):
        return pltpu.make_async_remote_copy(
            src_ref=src, dst_ref=dst, send_sem=send, recv_sem=recv, device_id=device, device_id_type=MESH
        )

    def halo_copy():
        return remote(ext.at[0:8], ext.at[32:40], halo_s.at[0], halo_r.at[0], (lax.rem(tm + 63, 64), 3))

    def z_copy(j):
        return remote(zall.at[0], zall.at[j], zs.at[j], zr.at[j], grp(j, 1))

    def z_forward(j):
        return remote(zall.at[j - 1], zall.at[j], zs.at[j], zr.at[j], grp(1, 1))

    def seg_copy(s):
        device = col(s, 1) if isinstance(s, int) else (tm, q)
        return remote(segs.at[0], segs.at[s], ss.at[s], sr.at[s], device)

    def part_copy(s, device=None):
        return remote(part.at[s], got.at[s], ps.at[s], pr.at[s], device or col(s, -1))

    def q_copy(j):
        return remote(qpart.at[j % 2], qgot.at[j], qs.at[j], qr.at[j], grp(j, -1))

    def last_copy(n, j):
        device = (col(28 + n, -1)[0], r_at[j])
        return remote(part.at[28 + n], last.at[4 * j + n], fs.at[4 * j + n], fr.at[4 * j + n], device)

    def final_copy(j):
        return remote(pall.at[0], pall.at[j], fs.at[16 + j], fr.at[16 + j], rep(j, 1))

    def each(low, high, do):
        lax.fori_loop(low, high, lambda i, c: (do(i), c)[1], 0)

    loads = [
        pltpu.make_async_copy(queries, rows_v, ls.at[0]),
        pltpu.make_async_copy(series, ext.at[0:32], ls.at[1]),
        pltpu.make_async_copy(tail, tail_v, ls.at[2]),
    ]
    for load in loads:
        load.start()

    barrier = pltpu.get_barrier_semaphore()

    def hello(device):
        pl.semaphore_signal(barrier, inc=1, device_id=device, device_id_type=MESH)

    for j in range(1, GROUP):
        hello(grp(j, 1))
    for s in range(1, COLUMN):
        hello(col(s, 1))
    hello((lax.rem(tm + 1, 64), r_at[2]))
    for j in range(1, REPLICAS):
        for n in range(4):
            hello((col(28 + n, 1)[0], r_at[j]))

    loads[0].wait()
    rows = rows_v[...]
    centered = rows - jnp.mean(rows, axis=1, keepdims=True)
    sigma = jnp.sqrt(jnp.mean(centered * centered, axis=1, keepdims=True) + 1e-05)
    zq = centered / sigma
    k = lax.broadcasted_iota(jnp.int32, (M, 384), 0)
    c = lax.broadcasted_iota(jnp.int32, (M, 384), 1)
    source = jnp.where(c < 128, 127 - c, jnp.where(c < 256, 383 - c, 287 - c % REST))
    order = (k == source).astype(jnp.bfloat16)
    zp = sum(jnp.dot(piece, order, preferred_element_type=jnp.float32) for piece in split(zq))
    lane = lax.broadcasted_iota(jnp.int32, (8, LANES), 1)
    quad = lane // REST
    packed = zp[24:32, 256:384]
    for g in range(3):
        packed = jnp.where(quad == g, zp[8 * g : 8 * g + 8, 256:384], packed)
    zall[0, 0:32] = zp[:, :128]
    zall[0, 32:64] = zp[:, 128:256]
    zall[0, 64:72] = packed
    loads[1].wait()
    loads[2].wait()

    @pl.when((q == 3) & (tm == 63))
    def _():
        ext[32:40] = jnp.zeros((8, LANES), jnp.float32)
        ext[32:33] = tail_v[0:128].reshape(1, LANES)
        ext[33:34] = tail_v[128:256].reshape(1, LANES)
        ext[34:35, 0 : REST - 1] = tail_v[256 : M - 1].reshape(1, REST - 1)

    def message():
        x = ext[pl.ds(pl.multiple_of(q * 8, 8), 16)]
        x = x - jnp.mean(x[0:8])
        segs[0, 0:16] = x
        segs[0, 16:24] = scales(x)

    @pl.when((q < 3) | (tm == 63))
    def _():
        message()

    pl.semaphore_wait(barrier, 1 + (GROUP - 1) + (COLUMN - 1) + 12)

    @pl.when((q == 1) & (tm > 0))
    def _():
        halo_copy().start()

    for j in (2, 6, 4, 1):
        z_copy(j).start()

    @pl.when((q == 3) & (tm < 63))
    def _():
        halo_copy().wait_recv()

    @pl.when((q == 3) & (tm < 63))
    def _():
        message()
    for s in range(1, COLUMN):
        seg_copy(s).start()
    acc[...] = jnp.full_like(acc, -1e30)

    def build(s, bh, bl, i):
        for u, block in hankel(lambda n: segs[s, n : n + 1], 10):
            bh[i, :, u * LANES : (u + 1) * LANES], bl[i, :, u * LANES : (u + 1) * LANES] = split(block)

    def compute(s, bh, bl, i, low=0, high=256):
        for t in range(SEG // 256):
            p = t * 256

            def two(ref):
                return [ref[i, :, p : p + 256], ref[i, :, p + 128 : p + 384]]

            def rest(ref):
                return ref[i, LANES - REST :, p + 256 : p + 512]

            h = jnp.concatenate(two(bh) + two(bh) + two(bl) + [rest(bh), rest(bh), rest(bl), rest(bh)], axis=0)
            out = jnp.dot(zcat[low:high], h, preferred_element_type=jnp.float32)
            best = jnp.max(out.reshape((high - low) // 8, 8, 256), axis=0)
            scaled = []
            for n in (0, 1):
                u, half = 2 * t + n, slice(n * LANES, (n + 1) * LANES)
                scale = segs[s, 16 + u : 17 + u]
                scaled.append(out[:, half] * scale)
                top = jnp.max(best[:, half], axis=0, keepdims=True) * scale
                part[s, u : u + 1] = jnp.maximum(part[s, u : u + 1], top) if low else top
            acc[low:high] = jnp.maximum(acc[low:high], jnp.maximum(*scaled))

    def take(j):
        at = slice(32 * (j // 2) + 128 * (j % 2), 32 * (j // 2) + 128 * (j % 2) + 32)
        total = jnp.zeros((32, 1), jnp.float32)
        for b in (0, 1):
            value = zall[j, 32 * b : 32 * b + 32]
            high, low = split(value)
            zcat[at, 128 * b : 128 * b + 128] = high
            zcat[at, 256 + 128 * b : 384 + 128 * b] = low
            zcat[at, 512 + 128 * b : 640 + 128 * b] = high
            total += jnp.sum(high.astype(jnp.float32) + low.astype(jnp.float32), axis=1, keepdims=True)
        four = []
        for g in range(4):
            value = jnp.where(quad == g, zall[j, 64:72], 0.0)
            value = value + pltpu.roll(value, 32, 1)
            four.append(value + pltpu.roll(value, 64, 1))
        value = jnp.concatenate(four, axis=0)
        high, low = split(value)
        high, low = high.astype(jnp.float32), low.astype(jnp.float32)
        lanes = lax.broadcasted_iota(jnp.int32, (32, LANES), 1)
        total += jnp.sum(jnp.where(lanes < REST, high + low, 0.0), axis=1, keepdims=True)
        part_of = lanes // REST
        mixed = jnp.where(part_of == 1, low, jnp.where(part_of == 3, total * (-1.0 / REST), high))
        zcat[at, 768:896] = mixed.astype(jnp.bfloat16)

    def four(s, last=False):
        compute(s, bha, bla, 0)
        build(s + 2, bhb, blb, 0)
        compute(s + 1, bha, bla, 1)
        build(s + 3, bhb, blb, 1)
        compute(s + 2, bhb, blb, 0)
        if not last:
            build(s + 4, bha, bla, 0)
        compute(s + 3, bhb, blb, 1)
        if not last:
            build(s + 5, bha, bla, 1)

    def fold(s):
        part_copy(s).wait_recv()
        found[...] = jnp.maximum(found[...], got[s])

    take(0)
    build(0, bha, bla, 0)
    for j in (2, 6, 4):
        z_copy(j).wait_recv()
        z_forward(j + 1).start()
        take(j)
    compute(0, bha, bla, 0, 0, 128)
    seg_copy(1).wait_recv()
    build(1, bha, bla, 1)
    compute(1, bha, bla, 1, 0, 128)
    z_copy(1).wait_recv()
    take(1)
    for j in (3, 7, 5):
        z_forward(j).wait_recv()
        take(j)
    for n in (2, 3, 4, 5):
        seg_copy(n).wait_recv()
    compute(0, bha, bla, 0, 128, 256)
    build(2, bhb, blb, 0)
    compute(1, bha, bla, 1, 128, 256)
    build(3, bhb, blb, 1)
    compute(2, bhb, blb, 0)
    build(4, bha, bla, 0)
    compute(3, bhb, blb, 1)
    build(5, bha, bla, 1)
    for n in (1, 2, 3):
        part_copy(n).start()
    found[...] = part[0]

    def step(i, carry):
        s = 8 * i + 4
        for h in (0, 4):
            for n in range(2, 6):
                seg_copy(s + h + n).wait_recv()
            four(s + h)
            for n in range(4):
                part_copy(s + h + n, place(2 * i + 1 + h // 4, n)).start()
        return carry

    lax.fori_loop(0, 3, step, 0)
    for n in (30, 31):
        seg_copy(n).wait_recv()
    four(28, last=True)
    for n in range(4):
        for j in range(REPLICAS):
            last_copy(n, j).start()

    best = jnp.max(jnp.transpose(acc[...]), axis=0, keepdims=True)
    qpart[0] = jnp.broadcast_to(best[:, :LANES], (8, LANES))
    qpart[1] = jnp.broadcast_to(best[:, LANES:], (8, LANES))
    for j in range(1, GROUP):
        q_copy(j).start()

    def distance(product):
        return jnp.sqrt(jnp.maximum(2.0 - 2.0 * product / M, 0.0))

    for n in range(1, 28):
        fold(n)
    pall[0] = found[...]
    for j in range(1, REPLICAS):
        final_copy(j).start()

    for j in range(1, GROUP):
        (z_forward(j) if j in (3, 5, 7) else z_copy(j)).wait_send()
    for n in range(1, COLUMN):
        seg_copy(n).wait_send()
    for n in range(1, 28):
        part_copy(n).wait_send()

    own = qpart[0, 0:1, 0:32]
    for j in range(1, GROUP):
        q_copy(j).wait_recv()
        own = jnp.maximum(own, qgot[j, 0:1, 32 * (j // 2) : 32 * (j // 2) + 32])
    qprof[...] = distance(own)

    for j in range(REPLICAS):
        for n in range(4):
            last_copy(n, j).wait_recv()
        if j:
            final_copy(j).wait_recv()
        best = jnp.maximum(pall[j], jnp.max(last[4 * j : 4 * j + 4], axis=0))
        at = pl.multiple_of(lax.rem(q - j + 4, 4) * 8, 8)
        prof[pl.ds(at, 8)] = distance(best)

    @pl.when((q == 1) & (tm > 0))
    def _():
        halo_copy().wait_send()

    for j in range(1, GROUP):
        q_copy(j).wait_send()
    for j in range(1, REPLICAS):
        final_copy(j).wait_send()
    for n in range(4):
        for j in range(REPLICAS):
            last_copy(n, j).wait_send()


def local(series, tail, queries):
    f32, bf16, dma = jnp.float32, jnp.bfloat16, pltpu.SemaphoreType.DMA
    vmem = pl.BlockSpec(memory_space=pltpu.VMEM)
    prof, qprof = pl.pallas_call(
        kernel,
        out_shape=[jax.ShapeDtypeStruct((32, LANES), f32), jax.ShapeDtypeStruct((1, 32), f32)],
        in_specs=[pl.BlockSpec(memory_space=pl.ANY)] * 3,
        out_specs=[vmem] * 2,
        scratch_shapes=[
            pltpu.VMEM((40, LANES), f32),
            pltpu.VMEM((M - 1,), f32),
            pltpu.VMEM((32, M), f32),
            pltpu.VMEM((COLUMN, 24, LANES), f32),
            pltpu.VMEM((2, LANES, 1280), bf16),
            pltpu.VMEM((2, LANES, 1280), bf16),
            pltpu.VMEM((2, LANES, 1280), bf16),
            pltpu.VMEM((2, LANES, 1280), bf16),
            pltpu.VMEM((GROUP, 72, LANES), f32),
            pltpu.VMEM((256, 896), bf16),
            pltpu.VMEM((256, LANES), f32),
            pltpu.VMEM((COLUMN, 8, LANES), f32),
            pltpu.VMEM((COLUMN, 8, LANES), f32),
            pltpu.VMEM((8, LANES), f32),
            pltpu.VMEM((2, 8, LANES), f32),
            pltpu.VMEM((GROUP, 8, LANES), f32),
            pltpu.VMEM((REPLICAS, 8, LANES), f32),
            pltpu.VMEM((4 * REPLICAS, 8, LANES), f32),
            dma((3,)), dma((1,)), dma((1,)),
            dma((GROUP,)), dma((GROUP,)),
            dma((COLUMN,)), dma((COLUMN,)),
            dma((COLUMN,)), dma((COLUMN,)),
            dma((GROUP,)), dma((GROUP,)),
            dma((20,)), dma((20,)),
        ],
        compiler_params=pltpu.CompilerParams(
            collective_id=0, has_side_effects=True, vmem_limit_bytes=60 * 2**20
        ),
    )(series.reshape(32, LANES), tail, queries)
    return prof.reshape(4096), qprof.reshape(32)


def solution(mesh):
    return jax.shard_map(
        local,
        mesh=mesh,
        in_specs=(P("tm"), P(), P(("tm", "query"), None)),
        out_specs=(P("tm"), P(("tm", "query"))),
        check_vma=False,
    )
```

```python
import jax
import jax.numpy as jnp
from jax import lax
from jax.experimental import pallas as pl
from jax.experimental.pallas import tpu as pltpu
from jax.sharding import PartitionSpec as P

M = 288
SEG = 1024
LANES = 128
COLUMN = 32
GROUP = 8
REPLICAS = 4
REST = M - 256
MESH = pl.DeviceIdType.MESH


def split(value):
    high = value.astype(jnp.bfloat16)
    low = (value - high.astype(jnp.float32)).astype(jnp.bfloat16)
    return high, low


def hankel(row, blocks):
    r = lax.broadcasted_iota(jnp.int32, (LANES, LANES), 0)
    lane = lax.broadcasted_iota(jnp.int32, (LANES, LANES), 1)
    this = pltpu.roll(jnp.broadcast_to(row(0), (LANES, LANES)), 1, 1, stride=1, stride_axis=0)
    for u in range(blocks):
        after = pltpu.roll(jnp.broadcast_to(row(u + 1), (LANES, LANES)), 1, 1, stride=1, stride_axis=0)
        yield u, jnp.where(lane <= r, this, after)
        this = after


def ahead(value, by):
    if by % LANES == 0:
        return pltpu.roll(value, 16 - by // LANES, 0)
    here = pltpu.roll(value, LANES - by, 1)
    lanes = lax.broadcasted_iota(jnp.int32, (16, LANES), 1)
    return jnp.where(lanes < LANES - by, here, pltpu.roll(here, 15, 0))


def scales(x):
    mean, dev, n = x, None, 1
    while n < 256:
        gap = ahead(mean, n) - mean
        joined = gap * gap * (n / 2)
        dev = joined if dev is None else dev + ahead(dev, n) + joined
        mean = mean + 0.5 * gap
        n *= 2
        if n == REST:
            mean_rest, dev_rest = mean, dev
    gap = ahead(mean_rest, 256) - mean
    dev = dev + ahead(dev_rest, 256) + gap * gap * (256 * REST / M)
    return 1.0 / jnp.sqrt(dev[0:8] / M + 1e-05)


def kernel(
    series, tail, queries, prof, qprof,
    ext, tail_v, rows_v, segs, bha, bla, bhb, blb, zall, zcat, acc, part, got, found, qpart, qgot, pall, last,
    ls, halo_s, halo_r, zs, zr, ss, sr, ps, pr, qs, qr, fs, fr,
):
    tm, q = lax.axis_index("tm"), lax.axis_index("query")
    zz, yy, xh = lax.div(tm, 8), lax.rem(lax.div(tm, 2), 4), lax.rem(tm, 2)
    xx, core = xh * 2 + lax.div(q, 2), lax.rem(q, 2)

    z_at = [lax.rem(zz + n, 8) * 8 for n in range(8)]
    y_at = [lax.rem(yy + n, 4) * 2 + xh for n in range(4)]
    x_at = [lax.rem(xx + n, 4) for n in range(4)]
    g_at = [tm - xh + lax.div(x, 2) for x in x_at]
    q_at = [[lax.rem(x, 2) * 2 + c for c in (core, 1 - core)] for x in x_at]
    r_at = [lax.rem(q + n, 4) for n in range(4)]

    def col(s, sign):
        return (z_at[sign * (s // 4) % 8] + y_at[sign * (s % 4) % 4], q)

    def place(b, n):
        return (lax.rem(zz - b + 8, 8) * 8 + y_at[-n % 4], q)

    def grp(j, sign):
        return (g_at[sign * (j // 2) % 4], q_at[sign * (j // 2) % 4][j % 2])

    def rep(j, sign):
        return (tm, r_at[sign * j % 4])

    def remote(src, dst, send, recv, device):
        return pltpu.make_async_remote_copy(
            src_ref=src, dst_ref=dst, send_sem=send, recv_sem=recv, device_id=device, device_id_type=MESH
        )

    def halo_copy():
        return remote(ext.at[0:8], ext.at[32:40], halo_s.at[0], halo_r.at[0], (lax.rem(tm + 63, 64), 3))

    def z_copy(j):
        return remote(zall.at[0], zall.at[j], zs.at[j], zr.at[j], grp(j, 1))

    def z_forward(j):
        return remote(zall.at[j - 1], zall.at[j], zs.at[j], zr.at[j], grp(1, 1))

    def seg_copy(s):
        device = col(s, 1) if isinstance(s, int) else (tm, q)
        return remote(segs.at[0], segs.at[s], ss.at[s], sr.at[s], device)

    def part_copy(s, device=None):
        return remote(part.at[s], got.at[s], ps.at[s], pr.at[s], device or col(s, -1))

    def q_copy(j):
        return remote(qpart.at[j % 2], qgot.at[j], qs.at[j], qr.at[j], grp(j, -1))

    def last_copy(n, j):
        device = (col(28 + n, -1)[0], r_at[j])
        return remote(part.at[28 + n], last.at[4 * j + n], fs.at[4 * j + n], fr.at[4 * j + n], device)

    def final_copy(j):
        return remote(pall.at[0], pall.at[j], fs.at[16 + j], fr.at[16 + j], rep(j, 1))

    def each(low, high, do):
        lax.fori_loop(low, high, lambda i, c: (do(i), c)[1], 0)

    loads = [
        pltpu.make_async_copy(queries, rows_v, ls.at[0]),
        pltpu.make_async_copy(series, ext.at[0:32], ls.at[1]),
        pltpu.make_async_copy(tail, tail_v, ls.at[2]),
    ]
    for load in loads:
        load.start()

    barrier = pltpu.get_barrier_semaphore()

    def hello(device):
        pl.semaphore_signal(barrier, inc=1, device_id=device, device_id_type=MESH)

    for j in range(1, GROUP):
        hello(grp(j, 1))
    for s in range(1, COLUMN):
        hello(col(s, 1))
    hello((lax.rem(tm + 1, 64), r_at[2]))
    for j in range(1, REPLICAS):
        for n in range(4):
            hello((col(28 + n, 1)[0], r_at[j]))

    loads[0].wait()
    rows = rows_v[...]
    centered = rows - jnp.mean(rows, axis=1, keepdims=True)
    sigma = jnp.sqrt(jnp.mean(centered * centered, axis=1, keepdims=True) + 1e-05)
    zq = centered / sigma
    k = lax.broadcasted_iota(jnp.int32, (M, 384), 0)
    c = lax.broadcasted_iota(jnp.int32, (M, 384), 1)
    source = jnp.where(c < 128, 127 - c, jnp.where(c < 256, 383 - c, 287 - c % REST))
    order = (k == source).astype(jnp.bfloat16)
    zp = sum(jnp.dot(piece, order, preferred_element_type=jnp.float32) for piece in split(zq))
    lane = lax.broadcasted_iota(jnp.int32, (8, LANES), 1)
    quad = lane // REST
    packed = zp[24:32, 256:384]
    for g in range(3):
        packed = jnp.where(quad == g, zp[8 * g : 8 * g + 8, 256:384], packed)
    zall[0, 0:32] = zp[:, :128]
    zall[0, 32:64] = zp[:, 128:256]
    zall[0, 64:72] = packed
    loads[1].wait()
    loads[2].wait()

    @pl.when((q == 3) & (tm == 63))
    def _():
        ext[32:40] = jnp.zeros((8, LANES), jnp.float32)
        ext[32:33] = tail_v[0:128].reshape(1, LANES)
        ext[33:34] = tail_v[128:256].reshape(1, LANES)
        ext[34:35, 0 : REST - 1] = tail_v[256 : M - 1].reshape(1, REST - 1)

    def message():
        x = ext[pl.ds(pl.multiple_of(q * 8, 8), 16)]
        x = x - jnp.mean(x[0:8])
        segs[0, 0:16] = x
        segs[0, 16:24] = scales(x)

    @pl.when((q < 3) | (tm == 63))
    def _():
        message()

    pl.semaphore_wait(barrier, 1 + (GROUP - 1) + (COLUMN - 1) + 12)

    @pl.when((q == 1) & (tm > 0))
    def _():
        halo_copy().start()

    for j in (2, 6, 4, 1):
        z_copy(j).start()

    @pl.when((q == 3) & (tm < 63))
    def _():
        halo_copy().wait_recv()

    @pl.when((q == 3) & (tm < 63))
    def _():
        message()
    for s in range(1, COLUMN):
        seg_copy(s).start()
    acc[...] = jnp.full_like(acc, -1e30)

    def build(s, bh, bl, i):
        for u, block in hankel(lambda n: segs[s, n : n + 1], 10):
            bh[i, :, u * LANES : (u + 1) * LANES], bl[i, :, u * LANES : (u + 1) * LANES] = split(block)

    def compute(s, bh, bl, i, low=0, high=256):
        for t in range(SEG // 256):
            p = t * 256

            def two(ref):
                return [ref[i, :, p : p + 256], ref[i, :, p + 128 : p + 384]]

            def rest(ref):
                return ref[i, LANES - REST :, p + 256 : p + 512]

            h = jnp.concatenate(two(bh) + two(bh) + two(bl) + [rest(bh), rest(bh), rest(bl), rest(bh)], axis=0)
            out = jnp.dot(zcat[low:high], h, preferred_element_type=jnp.float32)
            best = jnp.max(out.reshape((high - low) // 8, 8, 256), axis=0)
            scaled = []
            for n in (0, 1):
                u, half = 2 * t + n, slice(n * LANES, (n + 1) * LANES)
                scale = segs[s, 16 + u : 17 + u]
                scaled.append(out[:, half] * scale)
                top = jnp.max(best[:, half], axis=0, keepdims=True) * scale
                part[s, u : u + 1] = jnp.maximum(part[s, u : u + 1], top) if low else top
            acc[low:high] = jnp.maximum(acc[low:high], jnp.maximum(*scaled))

    def take(j):
        at = slice(32 * (j // 2) + 128 * (j % 2), 32 * (j // 2) + 128 * (j % 2) + 32)
        total = jnp.zeros((32, 1), jnp.float32)
        for b in (0, 1):
            value = zall[j, 32 * b : 32 * b + 32]
            high, low = split(value)
            zcat[at, 128 * b : 128 * b + 128] = high
            zcat[at, 256 + 128 * b : 384 + 128 * b] = low
            zcat[at, 512 + 128 * b : 640 + 128 * b] = high
            total += jnp.sum(high.astype(jnp.float32) + low.astype(jnp.float32), axis=1, keepdims=True)
        four = []
        for g in range(4):
            value = jnp.where(quad == g, zall[j, 64:72], 0.0)
            value = value + pltpu.roll(value, 32, 1)
            four.append(value + pltpu.roll(value, 64, 1))
        value = jnp.concatenate(four, axis=0)
        high, low = split(value)
        high, low = high.astype(jnp.float32), low.astype(jnp.float32)
        lanes = lax.broadcasted_iota(jnp.int32, (32, LANES), 1)
        total += jnp.sum(jnp.where(lanes < REST, high + low, 0.0), axis=1, keepdims=True)
        part_of = lanes // REST
        mixed = jnp.where(part_of == 1, low, jnp.where(part_of == 3, total * (-1.0 / REST), high))
        zcat[at, 768:896] = mixed.astype(jnp.bfloat16)

    def four(s, last=False):
        compute(s, bha, bla, 0)
        build(s + 2, bhb, blb, 0)
        compute(s + 1, bha, bla, 1)
        build(s + 3, bhb, blb, 1)
        compute(s + 2, bhb, blb, 0)
        if not last:
            build(s + 4, bha, bla, 0)
        compute(s + 3, bhb, blb, 1)
        if not last:
            build(s + 5, bha, bla, 1)

    def fold(s):
        part_copy(s).wait_recv()
        found[...] = jnp.maximum(found[...], got[s])

    take(0)
    build(0, bha, bla, 0)
    for j in (2, 6, 4):
        z_copy(j).wait_recv()
        z_forward(j + 1).start()
        take(j)
    compute(0, bha, bla, 0, 0, 128)
    z_copy(1).wait_recv()
    take(1)
    for j in (3, 7, 5):
        z_forward(j).wait_recv()
        take(j)
    for n in (1, 2, 3):
        seg_copy(n).wait_recv()
    build(1, bha, bla, 1)
    compute(0, bha, bla, 0, 128, 256)
    build(2, bhb, blb, 0)
    compute(1, bha, bla, 1)
    build(3, bhb, blb, 1)
    for n in (4, 5):
        seg_copy(n).wait_recv()
    compute(2, bhb, blb, 0)
    build(4, bha, bla, 0)
    compute(3, bhb, blb, 1)
    build(5, bha, bla, 1)
    for n in (1, 2, 3):
        part_copy(n).start()
    found[...] = part[0]

    def step(i, carry):
        s = 8 * i + 4
        for h in (0, 4):
            for n in range(2, 6):
                seg_copy(s + h + n).wait_recv()
            four(s + h)
            for n in range(4):
                part_copy(s + h + n, place(2 * i + 1 + h // 4, n)).start()
        return carry

    lax.fori_loop(0, 3, step, 0)
    for n in (30, 31):
        seg_copy(n).wait_recv()
    four(28, last=True)
    for n in range(4):
        for j in range(REPLICAS):
            last_copy(n, j).start()

    best = jnp.max(jnp.transpose(acc[...]), axis=0, keepdims=True)
    qpart[0] = jnp.broadcast_to(best[:, :LANES], (8, LANES))
    qpart[1] = jnp.broadcast_to(best[:, LANES:], (8, LANES))
    for j in range(1, GROUP):
        q_copy(j).start()

    def distance(product):
        return jnp.sqrt(jnp.maximum(2.0 - 2.0 * product / M, 0.0))

    for n in range(1, 28):
        fold(n)
    pall[0] = found[...]
    for j in range(1, REPLICAS):
        final_copy(j).start()

    for j in range(1, GROUP):
        (z_forward(j) if j in (3, 5, 7) else z_copy(j)).wait_send()
    for n in range(1, COLUMN):
        seg_copy(n).wait_send()
    for n in range(1, 28):
        part_copy(n).wait_send()

    own = qpart[0, 0:1, 0:32]
    for j in range(1, GROUP):
        q_copy(j).wait_recv()
        own = jnp.maximum(own, qgot[j, 0:1, 32 * (j // 2) : 32 * (j // 2) + 32])
    qprof[...] = distance(own)

    for j in range(REPLICAS):
        for n in range(4):
            last_copy(n, j).wait_recv()
        if j:
            final_copy(j).wait_recv()
        best = jnp.maximum(pall[j], jnp.max(last[4 * j : 4 * j + 4], axis=0))
        at = pl.multiple_of(lax.rem(q - j + 4, 4) * 8, 8)
        prof[pl.ds(at, 8)] = distance(best)

    @pl.when((q == 1) & (tm > 0))
    def _():
        halo_copy().wait_send()

    for j in range(1, GROUP):
        q_copy(j).wait_send()
    for j in range(1, REPLICAS):
        final_copy(j).wait_send()
    for n in range(4):
        for j in range(REPLICAS):
            last_copy(n, j).wait_send()


def local(series, tail, queries):
    f32, bf16, dma = jnp.float32, jnp.bfloat16, pltpu.SemaphoreType.DMA
    vmem = pl.BlockSpec(memory_space=pltpu.VMEM)
    prof, qprof = pl.pallas_call(
        kernel,
        out_shape=[jax.ShapeDtypeStruct((32, LANES), f32), jax.ShapeDtypeStruct((1, 32), f32)],
        in_specs=[pl.BlockSpec(memory_space=pl.ANY)] * 3,
        out_specs=[vmem] * 2,
        scratch_shapes=[
            pltpu.VMEM((40, LANES), f32),
            pltpu.VMEM((M - 1,), f32),
            pltpu.VMEM((32, M), f32),
            pltpu.VMEM((COLUMN, 24, LANES), f32),
            pltpu.VMEM((2, LANES, 1280), bf16),
            pltpu.VMEM((2, LANES, 1280), bf16),
            pltpu.VMEM((2, LANES, 1280), bf16),
            pltpu.VMEM((2, LANES, 1280), bf16),
            pltpu.VMEM((GROUP, 72, LANES), f32),
            pltpu.VMEM((256, 896), bf16),
            pltpu.VMEM((256, LANES), f32),
            pltpu.VMEM((COLUMN, 8, LANES), f32),
            pltpu.VMEM((COLUMN, 8, LANES), f32),
            pltpu.VMEM((8, LANES), f32),
            pltpu.VMEM((2, 8, LANES), f32),
            pltpu.VMEM((GROUP, 8, LANES), f32),
            pltpu.VMEM((REPLICAS, 8, LANES), f32),
            pltpu.VMEM((4 * REPLICAS, 8, LANES), f32),
            dma((3,)), dma((1,)), dma((1,)),
            dma((GROUP,)), dma((GROUP,)),
            dma((COLUMN,)), dma((COLUMN,)),
            dma((COLUMN,)), dma((COLUMN,)),
            dma((GROUP,)), dma((GROUP,)),
            dma((20,)), dma((20,)),
        ],
        compiler_params=pltpu.CompilerParams(
            collective_id=0, has_side_effects=True, vmem_limit_bytes=60 * 2**20
        ),
    )(series.reshape(32, LANES), tail, queries)
    return prof.reshape(4096), qprof.reshape(32)


def solution(mesh):
    return jax.shard_map(
        local,
        mesh=mesh,
        in_specs=(P("tm"), P(), P(("tm", "query"), None)),
        out_specs=(P("tm"), P(("tm", "query"))),
        check_vma=False,
    )
```
